32 devices in a mesh: dp: 4 (over z), pipe: 4 (over x, core), tensor: 2 (over y).
Axes of the slice: x: 2, y: 2, z: 4, core: 2. Of those that a mesh axis runs over, the one named last changes fastest.
Arguments:
- inputs: bfloat16 [2, 512, 8192], P(None, 'dp', 'tensor'), may hold values from -6 to 6
- cotangent: bfloat16 [2, 512, 8192], P(None, 'dp', 'tensor'), may hold values from -0.19921875 to 0.19921875
- up_weight: bfloat16 [4, 32, 6, 256, 256], P('pipe', 'tensor'), may hold values from -0.15625 to 0.15625
- down_weight: bfloat16 [4, 32, 6, 256, 256], P('pipe', 'tensor'), may hold values from -0.15625 to 0.15625
Outputs:
- up_grad: float32 [4, 32, 6, 256, 256], P('pipe', 'tensor')
- down_grad: float32 [4, 32, 6, 256, 256], P('pipe', 'tensor')
The draws below stay inside these ranges and needn't reach their ends.
All inputs are finite; a program needn't handle non-finite values.
Results may differ from the reference program's by a relative error of at most 0.02.
Values may be sent and summed in bfloat16 or wider, within the bound.
A program may use at most 192 MiB of HBM per device.

```python
import jax
import jax.numpy as jnp
from jax import lax

D = 8192
BS = 256
NB = 32
OFFS = 6
MICRO = 2
TOK = 512
LAYERS = 4


def steps_of(rng, dims, split, smallest, largest):
    gain, own = 1.0, jax.random.fold_in(rng, 6)
    for dim, shards_of in split:
        steps = jnp.exp(jax.random.uniform(jax.random.fold_in(own, dim), (shards_of,), jnp.float32, smallest / len(split), largest / len(split)))
        gain = gain * jnp.repeat(steps, dims[dim] // shards_of).reshape([-1 if axis == dim else 1 for axis in range(len(dims))])
    return gain


def noise(key, shape, deviation, bound, split=(), held_as=jnp.bfloat16):
    entries = deviation * jax.random.normal(key, shape, jnp.float32)
    if split:
        entries = entries * steps_of(key, shape, split, -0.22, 0.18)
    return jnp.clip(entries, -bound, bound).astype(held_as)


def setup_inputs(seed: int = 0) -> dict:
    key_of = jax.random.split(jax.random.key(seed), 5)
    return {
        "inputs": noise(key_of[0], (MICRO, TOK, D), 1.0, 6.0, ((1, 4), (2, 2))),
        "cotangent": noise(key_of[1], (MICRO, TOK, D), 0.03, 0.19921875, ((1, 4), (2, 2))),
        "up_weight": noise(key_of[2], (LAYERS, NB, OFFS, BS, BS), (OFFS * BS) ** -0.5, 0.15625, ((0, 4), (1, 2))),
        "down_weight": noise(key_of[3], (LAYERS, NB, OFFS, BS, BS), (OFFS * BS) ** -0.5, 0.15625, ((0, 4), (1, 2))),
    }


ROOT_HALF = 0.7071067811865476
INV_ROOT_TWO_PI = 0.3989422804014327


def offsets_table(count):
    return [0] + [2 ** j for j in range(count - 1)]


def gelu_value(v):
    return v * 0.5 * (1.0 + lax.erf(v * ROOT_HALF))


def gelu_slope(v):
    return 0.5 * (1.0 + lax.erf(v * ROOT_HALF)) + v * INV_ROOT_TWO_PI * jnp.exp(-0.5 * v * v)


def partner_index(blocks, count):
    rows_idx = jnp.arange(blocks, dtype=jnp.int32)[:, None]
    shifts = jnp.array(offsets_table(count), dtype=jnp.int32)[None, :]
    return jnp.bitwise_xor(rows_idx, shifts).astype(jnp.int32)


def butterfly(weight, values, index):
    gathered = values[:, index].astype(jnp.float32)
    return jnp.einsum("tnkb,nkbc->tnc", gathered, weight.astype(jnp.float32), precision=lax.Precision.HIGHEST)


def butterfly_t(weight, grads, index, columns):
    gathered = grads[:, index].astype(jnp.float32)
    moved = weight[index, columns].astype(jnp.float32)
    return jnp.einsum("tnkc,nkbc->tnb", gathered, moved, precision=lax.Precision.HIGHEST)


def outer_blocks(values, grads, index):
    gathered = values[:, index].astype(jnp.float32)
    return jnp.einsum("tnkb,tnc->nkbc", gathered, grads.astype(jnp.float32), precision=lax.Precision.HIGHEST)


def reference(inputs, cotangent, up_weight, down_weight):
    index = partner_index(NB, OFFS)
    columns = jnp.arange(OFFS, dtype=jnp.int32)[None, :]
    up_grad = jnp.zeros((LAYERS, NB, OFFS, BS, BS), jnp.float32)
    down_grad = jnp.zeros((LAYERS, NB, OFFS, BS, BS), jnp.float32)
    for micro_idx in range(MICRO):
        layer_in = inputs[micro_idx].reshape(TOK, NB, BS)
        saved_in, saved_hidden, saved_act = [], [], []
        for layer in range(LAYERS):
            hidden = butterfly(up_weight[layer], layer_in, index)
            act = gelu_value(hidden).astype(jnp.bfloat16)
            saved_in.append(layer_in)
            saved_hidden.append(hidden)
            saved_act.append(act)
            layer_in = (layer_in.astype(jnp.float32) + butterfly(down_weight[layer], act, index)).astype(jnp.bfloat16)
        grads = cotangent[micro_idx].reshape(TOK, NB, BS)
        for layer in range(LAYERS - 1, -1, -1):
            grad_act = butterfly_t(down_weight[layer], grads, index, columns)
            grad_hidden = (grad_act * gelu_slope(saved_hidden[layer])).astype(jnp.bfloat16)
            down_grad = down_grad.at[layer].add(outer_blocks(saved_act[layer], grads, index))
            up_grad = up_grad.at[layer].add(outer_blocks(saved_in[layer], grad_hidden, index))
            grads = (grads.astype(jnp.float32) + butterfly_t(up_weight[layer], grad_hidden, index, columns)).astype(jnp.bfloat16)
    return up_grad, down_grad
```

```python
import functools

import jax
import jax.numpy as jnp
from jax import lax
from jax.experimental import pallas as pl
from jax.experimental.pallas import tpu as pltpu
from jax.sharding import PartitionSpec as P

ROOT_HALF = 0.7071067811865476
INV_ROOT_TWO_PI = 0.3989422804014327
VMEM_LIMIT = 48 * 1024 * 1024


def offsets_table(count):
    return [0] + [2**j for j in range(count - 1)]


def split_offsets(count, width):
    table = list(enumerate(offsets_table(count)))
    local = [(k, s) for k, s in table if s < width]
    remote = [(k, s // width) for k, s in table if s >= width]
    return local, remote


def swapped(block, distance):
    count = lax.axis_size("tensor")
    return lax.ppermute(block, "tensor", [(i, i ^ distance) for i in range(count)])


def passed_along(x, by):
    size = lax.axis_size("pipe")
    return lax.ppermute(x, "pipe", [(i, i + by) for i in range(size) if 0 <= i + by < size])


def gelu_value(v):
    return v * 0.5 * (1.0 + lax.erf(v * ROOT_HALF))


def gelu_slope(v):
    return 0.5 * (1.0 + lax.erf(v * ROOT_HALF)) + v * INV_ROOT_TWO_PI * jnp.exp(-0.5 * v * v)


def apply_body(local, transpose, v_ref, *refs):
    w_refs, out_ref = refs[:-1], refs[-1]
    i = pl.program_id(0)
    dims = (((1,), (1 if transpose else 0,)), ((), ()))
    total = None
    for (_, s), w_ref in zip(local, w_refs):
        term = lax.dot_general(v_ref[i ^ s], w_ref[0, 0], dims, preferred_element_type=jnp.float32)
        total = term if total is None else total + term
    out_ref[0] = total


def weight_map(k, s, i):
    return (i ^ s, k, 0, 0)


def local_apply(v, w, local, transpose):
    blocks, tok, bs = v.shape
    return pl.pallas_call(
        functools.partial(apply_body, local, transpose),
        out_shape=jax.ShapeDtypeStruct(v.shape, jnp.float32),
        grid=(blocks,),
        in_specs=[pl.BlockSpec((blocks, tok, bs), lambda i: (0, 0, 0))]
        + [
            pl.BlockSpec((1, 1, bs, bs), functools.partial(weight_map, k, s if transpose else 0))
            for k, s in local
        ],
        out_specs=pl.BlockSpec((1, tok, bs), lambda i: (i, 0, 0)),
        compiler_params=pltpu.CompilerParams(vmem_limit_bytes=VMEM_LIMIT),
        cost_estimate=pl.CostEstimate(
            flops=2 * blocks * len(local) * tok * bs * bs,
            bytes_accessed=blocks * (len(local) * bs * bs * 2 + tok * bs * 6),
            transcendentals=0,
        ),
    )(v, *[w for _ in local])


def grad_body(local, remote, v_ref, g_ref, *refs):
    out_ref = refs[-1]
    i = pl.program_id(0)
    bs = g_ref.shape[-1]
    g = g_ref[...].reshape(-1, bs)
    dims = (((0,), (0,)), ((), ()))
    for k, s in local:
        v = v_ref[:, :, pl.ds(i ^ s, 1)].reshape(-1, bs)
        out_ref[0, k] = lax.dot_general(v, g, dims, preferred_element_type=jnp.float32)
    if remote:
        for pos, (k, _) in enumerate(remote):
            out_ref[0, k] = refs[0][pos, 0].astype(jnp.float32)


def weight_grad(v, g, summed, local, remote):
    dp, micro, blocks, tok, bs = v.shape
    count = len(local) + len(remote)
    in_specs = [
        pl.BlockSpec(v.shape, lambda i: (0, 0, 0, 0, 0)),
        pl.BlockSpec((dp, micro, 1, tok, bs), lambda i: (0, 0, i, 0, 0)),
    ]
    operands = [v, g]
    if remote:
        in_specs.append(pl.BlockSpec((len(remote), 1, bs, bs), lambda i: (0, i, 0, 0)))
        operands.append(summed)
    return pl.pallas_call(
        functools.partial(grad_body, local, remote),
        out_shape=jax.ShapeDtypeStruct((blocks, count, bs, bs), jnp.float32),
        grid=(blocks,),
        in_specs=in_specs,
        out_specs=pl.BlockSpec((1, count, bs, bs), lambda i: (i, 0, 0, 0)),
        compiler_params=pltpu.CompilerParams(vmem_limit_bytes=VMEM_LIMIT),
        cost_estimate=pl.CostEstimate(
            flops=2 * blocks * len(local) * dp * micro * tok * bs * bs,
            bytes_accessed=blocks * (count * bs * bs * 4 + dp * micro * tok * bs * 4),
            transcendentals=0,
        ),
    )(*operands)


def per_device(inputs, cotangent, up_weight, down_weight):
    w_up = up_weight[0]
    w_down = down_weight[0]
    blocks, count, bs = w_up.shape[0], w_up.shape[1], w_up.shape[2]
    micro, tok = inputs.shape[0], inputs.shape[1]
    segment = lax.axis_index("pipe")
    sections = lax.axis_size("pipe")
    steps = micro + sections - 1
    local, remote = split_offsets(count, blocks)

    def to_blocks(x):
        return x.reshape(micro, tok, blocks, bs).transpose(0, 2, 1, 3)

    inputs = to_blocks(inputs)
    cotangent = to_blocks(cotangent)

    def apply_forward(v, w):
        partners = [swapped(v, d) for _, d in remote]
        total = local_apply(v, w, local, False)
        for (k, _), partner in zip(remote, partners):
            total = total + jnp.einsum(
                "ltb,lbc->ltc", partner, w[:, k], preferred_element_type=jnp.float32
            )
        return total, partners

    def apply_transposed(g, w):
        sent = []
        for k, d in remote:
            term = jnp.einsum("ltc,lbc->ltb", g, w[:, k], preferred_element_type=jnp.float32)
            sent.append(swapped(term.astype(jnp.bfloat16), d))
        total = local_apply(g, w, local, True)
        for term in sent:
            total = total + term.astype(jnp.float32)
        return total

    kept = []
    outgoing = None
    for step in range(steps):
        own = inputs[min(step, micro - 1)]
        if step == 0:
            layer_in = own
        else:
            layer_in = jnp.where(segment == 0, own, passed_along(outgoing, 1))
        hidden, in_partners = apply_forward(layer_in, w_up)
        act = gelu_value(hidden).astype(jnp.bfloat16)
        mixed, act_partners = apply_forward(act, w_down)
        outgoing = (layer_in.astype(jnp.float32) + mixed).astype(jnp.bfloat16)
        kept.append((layer_in, act, hidden, in_partners, act_partners))

    kept = jax.tree.map(lambda *xs: jnp.stack(xs), *kept)
    own_kept = jax.tree.map(lambda x: lax.dynamic_slice_in_dim(x, segment, micro, 0), kept)
    z, act, hidden, z_partners, act_partners = own_kept
    z_all = lax.all_gather(z, "dp")
    act_all = lax.all_gather(act, "dp")

    made = []
    for step in range(steps):
        index = jnp.clip(step - (sections - 1 - segment), 0, micro - 1)
        own = cotangent[min(step, micro - 1)]
        if step == 0:
            grads = own
        else:
            grads = jnp.where(segment == sections - 1, own, passed_along(outgoing, -1))
        grad_act = apply_transposed(grads, w_down)
        slope = gelu_slope(lax.dynamic_index_in_dim(hidden, index, 0, keepdims=False))
        grad_hidden = (grad_act * slope).astype(jnp.bfloat16)
        made.append((grads, grad_hidden))
        if step < steps - 1:
            outgoing = (
                grads.astype(jnp.float32) + apply_transposed(grad_hidden, w_up)
            ).astype(jnp.bfloat16)

    made = jax.tree.map(lambda *xs: jnp.stack(xs), *made)
    g, grad_hidden = jax.tree.map(
        lambda x: lax.dynamic_slice_in_dim(x, sections - 1 - segment, micro, 0), made
    )
    g_all = lax.all_gather(g, "dp")
    grad_hidden_all = lax.all_gather(grad_hidden, "dp")

    up_sum = down_sum = None
    if remote:

        def remote_sum(partners, grads):
            return jnp.stack(
                [
                    jnp.einsum("mltb,mltc->lbc", p, grads, preferred_element_type=jnp.float32)
                    for p in partners
                ]
            ).astype(jnp.bfloat16)

        down_sum = lax.psum(remote_sum(act_partners, g), "dp")
        up_sum = lax.psum(remote_sum(z_partners, grad_hidden), "dp")
    grad_down = weight_grad(act_all, g_all, down_sum, local, remote)
    grad_up = weight_grad(z_all, grad_hidden_all, up_sum, local, remote)
    return grad_up[None], grad_down[None]


def solution(mesh):
    in_specs = (
        P(None, "dp", "tensor"),
        P(None, "dp", "tensor"),
        P("pipe", "tensor", None, None, None),
        P("pipe", "tensor", None, None, None),
    )
    out_specs = (P("pipe", "tensor", None, None, None), P("pipe", "tensor", None, None, None))
    return jax.shard_map(
        per_device, mesh=mesh, in_specs=in_specs, out_specs=out_specs, check_vma=False
    )
```

```python
import functools

import jax
import jax.numpy as jnp
from jax import lax
from jax.experimental import pallas as pl
from jax.experimental.pallas import tpu as pltpu
from jax.sharding import PartitionSpec as P

ROOT_HALF = 0.7071067811865476
INV_ROOT_TWO_PI = 0.3989422804014327
VMEM_LIMIT = 48 * 1024 * 1024


def offsets_table(count):
    return [0] + [2**j for j in range(count - 1)]


def split_offsets(count, width):
    table = list(enumerate(offsets_table(count)))
    local = [(k, s) for k, s in table if s < width]
    remote = [(k, s // width) for k, s in table if s >= width]
    return local, remote


def swapped(block, distance):
    count = lax.axis_size("tensor")
    return lax.ppermute(block, "tensor", [(i, i ^ distance) for i in range(count)])


def passed_along(x, by):
    size = lax.axis_size("pipe")
    return lax.ppermute(x, "pipe", [(i, i + by) for i in range(size) if 0 <= i + by < size])


def gelu_value(v):
    return v * 0.5 * (1.0 + lax.erf(v * ROOT_HALF))


def gelu_slope(v):
    return 0.5 * (1.0 + lax.erf(v * ROOT_HALF)) + v * INV_ROOT_TWO_PI * jnp.exp(-0.5 * v * v)


def apply_body(local, transpose, v_ref, *refs):
    w_refs, out_ref = refs[: len(local)], refs[-1]
    i = pl.program_id(0)
    dims = (((1,), (1 if transpose else 0,)), ((), ()))
    total = None
    for (_, s), w_ref in zip(local, w_refs):
        term = lax.dot_general(v_ref[i ^ s], w_ref[0, 0], dims, preferred_element_type=jnp.float32)
        total = term if total is None else total + term
    out_ref[0] = total


def weight_map(k, s, i):
    return (i ^ s, k, 0, 0)


def local_apply(v, w, local, transpose, after=()):
    blocks, tok, bs = v.shape
    return pl.pallas_call(
        functools.partial(apply_body, local, transpose),
        out_shape=jax.ShapeDtypeStruct(v.shape, jnp.float32),
        grid=(blocks,),
        in_specs=[pl.BlockSpec((blocks, tok, bs), lambda i: (0, 0, 0))]
        + [
            pl.BlockSpec((1, 1, bs, bs), functools.partial(weight_map, k, s if transpose else 0))
            for k, s in local
        ]
        + [pl.BlockSpec(memory_space=pl.ANY) for _ in after],
        out_specs=pl.BlockSpec((1, tok, bs), lambda i: (i, 0, 0)),
        compiler_params=pltpu.CompilerParams(vmem_limit_bytes=VMEM_LIMIT),
        cost_estimate=pl.CostEstimate(
            flops=2 * blocks * len(local) * tok * bs * bs,
            bytes_accessed=blocks * (len(local) * bs * bs * 2 + tok * bs * 6),
            transcendentals=0,
        ),
    )(v, *[w for _ in local], *after)


def grad_body(local, remote, micro, *refs):
    g_refs, v_refs, out_ref = refs[:micro], refs[micro : 2 * micro], refs[-1]
    partner_refs = refs[2 * micro : -1]
    i = pl.program_id(0)
    bs = out_ref.shape[-1]
    grads = [g[...].reshape(-1, bs) for g in g_refs]
    dims = (((0,), (0,)), ((), ()))

    def product(values):
        total = None
        for v, g in zip(values, grads):
            term = lax.dot_general(v, g, dims, preferred_element_type=jnp.float32)
            total = term if total is None else total + term
        return total

    for k, s in local:
        out_ref[0, k] = product([v[:, pl.ds(i ^ s, 1)].reshape(-1, bs) for v in v_refs])
    for pos, (k, _) in enumerate(remote):
        own = partner_refs[pos * micro : (pos + 1) * micro]
        out_ref[0, k] = product([v[...].reshape(-1, bs) for v in own])


def weight_grad(values, grads, partners, local, remote):
    micro = len(values)
    dp, blocks, tok, bs = values[0].shape
    count = len(local) + len(remote)
    one = pl.BlockSpec((dp, 1, tok, bs), lambda i: (0, i, 0, 0))
    whole = pl.BlockSpec((dp, blocks, tok, bs), lambda i: (0, 0, 0, 0))
    return pl.pallas_call(
        functools.partial(grad_body, local, remote, micro),
        out_shape=jax.ShapeDtypeStruct((blocks, count, bs, bs), jnp.float32),
        grid=(blocks,),
        in_specs=[one] * micro + [whole] * micro + [one] * (micro * len(remote)),
        out_specs=pl.BlockSpec((1, count, bs, bs), lambda i: (i, 0, 0, 0)),
        compiler_params=pltpu.CompilerParams(vmem_limit_bytes=VMEM_LIMIT),
        cost_estimate=pl.CostEstimate(
            flops=2 * blocks * count * dp * micro * tok * bs * bs,
            bytes_accessed=blocks * (count * bs * bs * 4 + dp * micro * tok * bs * 4),
            transcendentals=0,
        ),
    )(*grads, *values, *[p for group in partners for p in group])


def per_device(inputs, cotangent, up_weight, down_weight):
    w_up = up_weight[0]
    w_down = down_weight[0]
    blocks, count, bs = w_up.shape[0], w_up.shape[1], w_up.shape[2]
    micro, tok = inputs.shape[0], inputs.shape[1]
    segment = lax.axis_index("pipe")
    sections = lax.axis_size("pipe")
    steps = micro + sections - 1
    local, remote = split_offsets(count, blocks)

    def to_blocks(x):
        return x.reshape(micro, tok, blocks, bs).transpose(0, 2, 1, 3)

    inputs = to_blocks(inputs)
    cotangent = to_blocks(cotangent)

    def apply_forward(v, w):
        partners = [swapped(v, d) for _, d in remote]
        total = local_apply(v, w, local, False)
        for (k, _), partner in zip(remote, partners):
            total = total + jnp.einsum(
                "ltb,lbc->ltc", partner, w[:, k], preferred_element_type=jnp.float32
            )
        return total

    def apply_transposed(g, w, after=()):
        sent = []
        for k, d in remote:
            term = jnp.einsum("ltc,lbc->ltb", g, w[:, k], preferred_element_type=jnp.float32)
            sent.append(swapped(term.astype(jnp.bfloat16), d))
        total = local_apply(g, w, local, True, after)
        for term in sent:
            total = total + term.astype(jnp.float32)
        return total

    kept = []
    outgoing = None
    for step in range(steps):
        own = inputs[min(step, micro - 1)]
        if step == 0:
            layer_in = own
        else:
            layer_in = jnp.where(segment == 0, own, passed_along(outgoing, 1))
        hidden = apply_forward(layer_in, w_up)
        act = gelu_value(hidden).astype(jnp.bfloat16)
        mixed = apply_forward(act, w_down)
        outgoing = (layer_in.astype(jnp.float32) + mixed).astype(jnp.bfloat16)
        kept.append((layer_in, act, hidden))

    def own_step(items, first, m):
        window = items[m : m + sections]
        return lax.dynamic_index_in_dim(jnp.stack(window), first, 0, keepdims=False)

    def gathered(x):
        return lax.all_gather(x, "dp")

    z_all, act_all = [], []
    for m in range(micro):
        z_all.append(gathered(own_step([x[0] for x in kept], segment, m)))
        act_all.append(gathered(own_step([x[1] for x in kept], segment, m)))
    hidden = jnp.stack([own_step([x[2] for x in kept], segment, m) for m in range(micro)])
    due = [x for pair in zip(z_all, act_all) for x in pair]

    made = []
    for step in range(steps):
        index = jnp.clip(step - (sections - 1 - segment), 0, micro - 1)
        own = cotangent[min(step, micro - 1)]
        if step == 0:
            grads = own
        else:
            grads = jnp.where(segment == sections - 1, own, passed_along(outgoing, -1))
        after = due[step - 1 : step] if step < steps - 1 else due[step - 1 :]
        grad_act = apply_transposed(grads, w_down, after if step else ())
        slope = gelu_slope(lax.dynamic_index_in_dim(hidden, index, 0, keepdims=False))
        grad_hidden = (grad_act * slope).astype(jnp.bfloat16)
        made.append((grads, grad_hidden))
        if step < steps - 1:
            outgoing = (
                grads.astype(jnp.float32) + apply_transposed(grad_hidden, w_up)
            ).astype(jnp.bfloat16)

    g_all, grad_hidden_all = [], []
    last = sections - 1 - segment
    for m in range(micro):
        g_all.append(gathered(own_step([x[0] for x in made], last, m)))
        grad_hidden_all.append(gathered(own_step([x[1] for x in made], last, m)))

    act_partners = [[swapped(x, d) for x in act_all] for _, d in remote]
    z_partners = [[swapped(x, d) for x in z_all] for _, d in remote]
    grad_down = weight_grad(act_all, g_all, act_partners, local, remote)
    grad_up = weight_grad(z_all, grad_hidden_all, z_partners, local, remote)
    return grad_up[None], grad_down[None]


def solution(mesh):
    in_specs = (
        P(None, "dp", "tensor"),
        P(None, "dp", "tensor"),
        P("pipe", "tensor", None, None, None),
        P("pipe", "tensor", None, None, None),
    )
    out_specs = (P("pipe", "tensor", None, None, None), P("pipe", "tensor", None, None, None))
    return jax.shard_map(
        per_device, mesh=mesh, in_specs=in_specs, out_specs=out_specs, check_vma=False
    )
```

```python
import functools

import jax
import jax.numpy as jnp
from jax import lax
from jax.experimental import pallas as pl
from jax.experimental.pallas import tpu as pltpu
from jax.sharding import PartitionSpec as P

ROOT_HALF = 0.7071067811865476
INV_ROOT_TWO_PI = 0.3989422804014327
VMEM_LIMIT = 48 * 1024 * 1024


def offsets_table(count):
    return [0] + [2**j for j in range(count - 1)]


def split_offsets(count, width):
    table = list(enumerate(offsets_table(count)))
    local = [(k, s) for k, s in table if s < width]
    remote = [(k, s // width) for k, s in table if s >= width]
    return local, remote


def swapped(block, distance, pipes=None):
    count = lax.axis_size("tensor")
    if pipes is None:
        pipes = range(lax.axis_size("pipe"))
    pairs = [(p * count + i, p * count + (i ^ distance)) for p in pipes for i in range(count)]
    return lax.ppermute(block, ("pipe", "tensor"), pairs)


def passed_along(x, by):
    size = lax.axis_size("pipe")
    return lax.ppermute(x, "pipe", [(i, i + by) for i in range(size) if 0 <= i + by < size])


def gelu_value(v):
    return v * 0.5 * (1.0 + lax.erf(v * ROOT_HALF))


def gelu_slope(v):
    return 0.5 * (1.0 + lax.erf(v * ROOT_HALF)) + v * INV_ROOT_TWO_PI * jnp.exp(-0.5 * v * v)


def apply_body(local, transpose, v_ref, *refs):
    w_refs, out_ref = refs[: len(local)], refs[-1]
    i = pl.program_id(0)
    dims = (((1,), (1 if transpose else 0,)), ((), ()))
    total = None
    for (_, s), w_ref in zip(local, w_refs):
        term = lax.dot_general(v_ref[i ^ s], w_ref[0, 0], dims, preferred_element_type=jnp.float32)
        total = term if total is None else total + term
    out_ref[0] = total


def weight_map(k, s, i):
    return (i ^ s, k, 0, 0)


def local_apply(v, w, local, transpose, after=()):
    blocks, tok, bs = v.shape
    return pl.pallas_call(
        functools.partial(apply_body, local, transpose),
        out_shape=jax.ShapeDtypeStruct(v.shape, jnp.float32),
        grid=(blocks,),
        in_specs=[pl.BlockSpec((blocks, tok, bs), lambda i: (0, 0, 0))]
        + [
            pl.BlockSpec((1, 1, bs, bs), functools.partial(weight_map, k, s if transpose else 0))
            for k, s in local
        ]
        + [pl.BlockSpec(memory_space=pl.ANY) for _ in after],
        out_specs=pl.BlockSpec((1, tok, bs), lambda i: (i, 0, 0)),
        compiler_params=pltpu.CompilerParams(vmem_limit_bytes=VMEM_LIMIT),
        cost_estimate=pl.CostEstimate(
            flops=2 * blocks * len(local) * tok * bs * bs,
            bytes_accessed=blocks * (len(local) * bs * bs * 2 + tok * bs * 6),
            transcendentals=0,
        ),
    )(v, *[w for _ in local], *after)


def grad_body(local, remote, micro, *refs):
    g_refs, v_refs, out_ref = refs[:micro], refs[micro : 2 * micro], refs[-1]
    partner_refs = refs[2 * micro : -1]
    i = pl.program_id(0)
    bs = out_ref.shape[-1]
    grads = [g[...].reshape(-1, bs) for g in g_refs]
    dims = (((0,), (0,)), ((), ()))

    def product(values):
        total = None
        for v, g in zip(values, grads):
            term = lax.dot_general(v, g, dims, preferred_element_type=jnp.float32)
            total = term if total is None else total + term
        return total

    for k, s in local:
        out_ref[0, k] = product([v[:, pl.ds(i ^ s, 1)].reshape(-1, bs) for v in v_refs])
    for pos, (k, _) in enumerate(remote):
        own = partner_refs[pos * micro : (pos + 1) * micro]
        out_ref[0, k] = product([v[...].reshape(-1, bs) for v in own])


def weight_grad(values, grads, partners, local, remote):
    micro = len(values)
    dp, blocks, tok, bs = values[0].shape
    count = len(local) + len(remote)
    one = pl.BlockSpec((dp, 1, tok, bs), lambda i: (0, i, 0, 0))
    whole = pl.BlockSpec((dp, blocks, tok, bs), lambda i: (0, 0, 0, 0))
    return pl.pallas_call(
        functools.partial(grad_body, local, remote, micro),
        out_shape=jax.ShapeDtypeStruct((blocks, count, bs, bs), jnp.float32),
        grid=(blocks,),
        in_specs=[one] * micro + [whole] * micro + [one] * (micro * len(remote)),
        out_specs=pl.BlockSpec((1, count, bs, bs), lambda i: (i, 0, 0, 0)),
        compiler_params=pltpu.CompilerParams(vmem_limit_bytes=VMEM_LIMIT),
        cost_estimate=pl.CostEstimate(
            flops=2 * blocks * count * dp * micro * tok * bs * bs,
            bytes_accessed=blocks * (count * bs * bs * 4 + dp * micro * tok * bs * 4),
            transcendentals=0,
        ),
    )(*grads, *values, *[p for group in partners for p in group])


def per_device(inputs, cotangent, up_weight, down_weight):
    w_up = up_weight[0]
    w_down = down_weight[0]
    blocks, count, bs = w_up.shape[0], w_up.shape[1], w_up.shape[2]
    micro, tok = inputs.shape[0], inputs.shape[1]
    segment = lax.axis_index("pipe")
    sections = lax.axis_size("pipe")
    steps = micro + sections - 1
    local, remote = split_offsets(count, blocks)

    def to_blocks(x):
        return x.reshape(micro, tok, blocks, bs).transpose(0, 2, 1, 3)

    inputs = to_blocks(inputs)
    cotangent = to_blocks(cotangent)

    def working(step, sections_in_order):
        return [p for pos, p in enumerate(sections_in_order) if 0 <= step - pos < micro]

    def apply_forward(v, w, pipes):
        partners = [swapped(v, d, pipes) for _, d in remote]
        total = local_apply(v, w, local, False)
        for (k, _), partner in zip(remote, partners):
            total = total + jnp.einsum(
                "ltb,lbc->ltc", partner, w[:, k], preferred_element_type=jnp.float32
            )
        return total

    def apply_transposed(g, w, pipes, after=()):
        sent = []
        for k, d in remote:
            term = jnp.einsum("ltc,lbc->ltb", g, w[:, k], preferred_element_type=jnp.float32)
            sent.append(swapped(term.astype(jnp.bfloat16), d, pipes))
        total = local_apply(g, w, local, True, after)
        for term in sent:
            total = total + term.astype(jnp.float32)
        return total

    kept = []
    outgoing = None
    for step in range(steps):
        own = inputs[min(step, micro - 1)]
        if step == 0:
            layer_in = own
        else:
            layer_in = jnp.where(segment == 0, own, passed_along(outgoing, 1))
        pipes = working(step, range(sections))
        hidden = apply_forward(layer_in, w_up, pipes)
        act = gelu_value(hidden).astype(jnp.bfloat16)
        kept.append((layer_in, act, hidden))
        if step < steps - 1:
            onward = [p for p in pipes if p < sections - 1]
            mixed = apply_forward(act, w_down, onward)
            outgoing = (layer_in.astype(jnp.float32) + mixed).astype(jnp.bfloat16)

    def own_step(items, first, m):
        window = items[m : m + sections]
        return lax.dynamic_index_in_dim(jnp.stack(window), first, 0, keepdims=False)

    def gathered(x):
        return lax.all_gather(x, "dp")

    z_all, act_all = [], []
    for m in range(micro):
        z_all.append(gathered(own_step([x[0] for x in kept], segment, m)))
        act_all.append(gathered(own_step([x[1] for x in kept], segment, m)))
    hidden = jnp.stack([own_step([x[2] for x in kept], segment, m) for m in range(micro)])
    due = {}
    for pos, x in enumerate([x for pair in zip(z_all, act_all) for x in pair]):
        due.setdefault(3 * pos, []).append(x)
    z_partners = [[swapped(x, d) for x in z_all] for _, d in remote]
    act_partners = [[swapped(x, d) for x in act_all] for _, d in remote]
    due.setdefault(2 * steps - 2, []).extend(group[0] for group in z_partners)

    made = []
    for step in range(steps):
        index = jnp.clip(step - (sections - 1 - segment), 0, micro - 1)
        own = cotangent[min(step, micro - 1)]
        if step == 0:
            grads = own
        else:
            grads = jnp.where(segment == sections - 1, own, passed_along(outgoing, -1))
        pipes = working(step, range(sections - 1, -1, -1))
        grad_act = apply_transposed(grads, w_down, pipes, due.get(2 * step, ()))
        slope = gelu_slope(lax.dynamic_index_in_dim(hidden, index, 0, keepdims=False))
        grad_hidden = (grad_act * slope).astype(jnp.bfloat16)
        made.append((grads, grad_hidden))
        if step < steps - 1:
            onward = [p for p in pipes if p > 0]
            passed = apply_transposed(grad_hidden, w_up, onward, due.get(2 * step + 1, ()))
            outgoing = (grads.astype(jnp.float32) + passed).astype(jnp.bfloat16)

    g_all, grad_hidden_all = [], []
    last = sections - 1 - segment
    for m in range(micro):
        g_all.append(gathered(own_step([x[0] for x in made], last, m)))
        grad_hidden_all.append(gathered(own_step([x[1] for x in made], last, m)))

    grad_down = weight_grad(act_all, g_all, act_partners, local, remote)
    grad_up = weight_grad(z_all, grad_hidden_all, z_partners, local, remote)
    return grad_up[None], grad_down[None]


def solution(mesh):
    in_specs = (
        P(None, "dp", "tensor"),
        P(None, "dp", "tensor"),
        P("pipe", "tensor", None, None, None),
        P("pipe", "tensor", None, None, None),
    )
    out_specs = (P("pipe", "tensor", None, None, None), P("pipe", "tensor", None, None, None))
    return jax.shard_map(
        per_device, mesh=mesh, in_specs=in_specs, out_specs=out_specs, check_vma=False
    )
```
